32 devices in a mesh: grp: 2 (over x), wide: 16 (over z, y, core).
Axes of the slice: x: 2, y: 2, z: 4, core: 2. Of those that a mesh axis runs over, the one named last changes fastest.
Arguments:
- homolog_stack_state: bfloat16 [256, 128, 256], P(('grp', 'wide')), parts along dimension 0, may hold values from -6 to 6
- present_flags: int32 [256, 128], P('grp'), parts along dimension 0, may hold values from 0 to 1, as said below
- chain_ordinal_labels: int32 [256], P('grp'), parts along dimension 0, may hold values from 0 to 383, as said below
- pairwise_repr: bfloat16 [256, 128, 128], P(('grp', 'wide')), parts along dimension 0, may hold values from -6 to 6
- heeding_normalizer_gains: float32 [256], replicated, may hold values from 0.1 to 1.9
- retrieval_weights_qkv: bfloat16 [256, 768], replicated, may hold values from -2.7308912 to 2.7308912
- logistic_weights: bfloat16 [256, 256], replicated, may hold values from -0.375 to 0.375
- logistic_intercept: float32 [256], replicated, may hold values from -4 to 4
- emitted_weights: bfloat16 [256, 256], replicated, may hold values from -0.375 to 0.375
- dyadic_normalizer_gains: float32 [256], replicated, may hold values from 0.1 to 1.9
- former_operand_weights: bfloat16 [256, 32], replicated, may hold values from -0.375 to 0.375
- latter_operand_weights: bfloat16 [256, 32], replicated, may hold values from -0.375 to 0.375
- flattened_outer_projection: bfloat16 [1024, 128], replicated, may hold values from -0.75 to 0.75
- clipped_separation_embedding: bfloat16 [65, 128], replicated, may hold values from -5 to 5
Outputs:
- homolog_changed: bfloat16 [256, 128, 256], P(('grp', 'wide')), parts along dimension 0
- couple_state_changed: bfloat16 [256, 128, 128], P(('grp', 'wide')), parts along dimension 0
The draws below stay inside these ranges and needn't reach their ends.
There are 2 independent parts, one for each index of `grp`. The reference program is written for one: setup_inputs(seed, part) draws one part's arguments, and reference() takes and returns one part's arrays. A program takes and returns all parts, laid end to end along the dimension named above; an argument that names none is the same for every part. Nothing has to cross between parts.
Inputs may be any that keep to these rules, and one draw needn't show every extreme that they name: `present_flags`: every entry of the first sequence is 1. `chain_ordinal_labels`: rises from token to token by 1 to 3.
All inputs are finite; a program needn't handle non-finite values.
Results may differ from the reference program's by a relative error of at most 0.0094.
The reference program's roundings to bfloat16 on the way count: a program that leaves them out, or rounds other values in their place, can miss the bound.
Values may be sent and summed in bfloat16 or wider, within the bound.
A program may use at most 128 MiB of HBM per device.

```python
import math
import jax
import jax.numpy as jnp
from jax import lax

HOMOLOG_CHANNELS = 256
HEAD_TOTAL = 8
OPERAND_BREADTH = 32
PAIR_WIDTH = 128
RELPOS_CLIP = 32
HOMOLOG_TOTAL = 128
HEAD_SIZE = 32
STRETCH_SIZE = 128


def draw_retrieval_weights_qkv(key, part):
    starting_amount = jnp.clip(jax.random.normal(key, (HOMOLOG_CHANNELS, 3, HOMOLOG_CHANNELS), jnp.float32), -6.0, 6.0)
    starting_amount = starting_amount / math.sqrt(HOMOLOG_CHANNELS)
    return starting_amount.reshape(HOMOLOG_CHANNELS, 3 * HOMOLOG_CHANNELS).astype(jnp.bfloat16)


def draw_present_flags(key, part):
    probe_occurrences = jax.random.fold_in(key, 11)
    probe_element = jax.random.fold_in(key, 12)
    speed_quantities = jax.random.randint(probe_occurrences, (HOMOLOG_TOTAL, 1), 2, 9)
    grid_quantities = jax.random.randint(probe_element, (HOMOLOG_TOTAL, STRETCH_SIZE), 0, 8)
    live = (grid_quantities < speed_quantities).astype(jnp.int32)
    leading_element = (lax.broadcasted_iota(jnp.int32, (HOMOLOG_TOTAL, STRETCH_SIZE), 0) == 0).astype(jnp.int32)
    return jnp.maximum(live, leading_element)


def draw_chain_ordinal_labels(key, part):
    key_step = jax.random.fold_in(key, 21)
    gaps = jax.random.randint(key_step, (STRETCH_SIZE,), 1, 4).astype(jnp.int32)
    running = jnp.cumsum(gaps).astype(jnp.int32)
    after = running[STRETCH_SIZE - 1] - running
    return (3 * STRETCH_SIZE - 1 - after).astype(jnp.int32)


def shard_levels(key, shape, shards, least, largest):
    loudness, own = 1.0, jax.random.fold_in(key, 6)
    for axis_at, blocks in shards:
        draws = jnp.exp(jax.random.uniform(jax.random.fold_in(own, axis_at), (blocks,), jnp.float32, least / len(shards), largest / len(shards)))
        loudness = loudness * jnp.repeat(draws, shape[axis_at] // blocks).reshape([-1 if axis == axis_at else 1 for axis in range(len(shape))])
    return loudness


def noise(stream_key, dims, deviation, bound, cuts=(), held_as=jnp.bfloat16):
    entries = jax.random.normal(stream_key, dims, jnp.float32) * deviation
    if len(cuts) > 0:
        entries = shard_levels(stream_key, dims, cuts, -0.22, 0.18) * entries
    return jnp.clip(entries, min=-bound, max=bound).astype(held_as)


def setup_inputs(seed: int = 0, part: int = 0) -> dict:
    key_of = jax.random.split(jax.random.key(seed), 15)
    own_keys = jax.random.split(jax.random.fold_in(key_of[14], part), 15)
    return {
        "homolog_stack_state": noise(own_keys[0], (HOMOLOG_TOTAL, STRETCH_SIZE, HOMOLOG_CHANNELS), 1.0, 6.0, ((0, 16),)),
        "present_flags": draw_present_flags(jax.random.fold_in(jax.random.fold_in(key_of[14], part), 71), part),
        "chain_ordinal_labels": draw_chain_ordinal_labels(jax.random.fold_in(jax.random.fold_in(key_of[14], part), 71), part),
        "pairwise_repr": noise(own_keys[3], (STRETCH_SIZE, STRETCH_SIZE, PAIR_WIDTH), 1.0, 6.0, ((0, 16),)),
        "heeding_normalizer_gains": jnp.clip(1.0 + 0.18 * jax.random.normal(key_of[4], (HOMOLOG_CHANNELS,), jnp.float32), 0.1, 1.9),
        "retrieval_weights_qkv": draw_retrieval_weights_qkv(jax.random.fold_in(key_of[14], 71), part),
        "logistic_weights": noise(key_of[6], (HOMOLOG_CHANNELS, HOMOLOG_CHANNELS), HOMOLOG_CHANNELS ** -0.5, 0.375),
        "logistic_intercept": noise(key_of[7], (HOMOLOG_CHANNELS,), 1.0, 4.0, (), jnp.float32),
        "emitted_weights": noise(key_of[8], (HOMOLOG_CHANNELS, HOMOLOG_CHANNELS), HOMOLOG_CHANNELS ** -0.5, 0.375),
        "dyadic_normalizer_gains": jnp.clip(1.0 + 0.18 * jax.random.normal(key_of[9], (HOMOLOG_CHANNELS,), jnp.float32), 0.1, 1.9),
        "former_operand_weights": noise(key_of[10], (HOMOLOG_CHANNELS, OPERAND_BREADTH), HOMOLOG_CHANNELS ** -0.5, 0.375),
        "latter_operand_weights": noise(key_of[11], (HOMOLOG_CHANNELS, OPERAND_BREADTH), HOMOLOG_CHANNELS ** -0.5, 0.375),
        "flattened_outer_projection": noise(key_of[12], (OPERAND_BREADTH * OPERAND_BREADTH, PAIR_WIDTH), (2 * OPERAND_BREADTH) ** -0.5, 0.75),
        "clipped_separation_embedding": noise(key_of[13], (2 * RELPOS_CLIP + 1, PAIR_WIDTH), 1.0, 5.0),
    }


epsilon = 1e-05

def standardize_features(values, gain_vector):
    mean = lax.optimization_barrier(jnp.mean(values, axis=-1, keepdims=True))
    centered = values - mean
    variance = lax.optimization_barrier(jnp.mean(centered * centered, axis=-1, keepdims=True))
    return centered * lax.rsqrt(variance + epsilon) * gain_vector.astype(jnp.float32)

def downward_heeding_blend(homolog_stack_state, presence_tally, heeding_normalizer_gains, retrieval_weights_qkv, logistic_weights, logistic_intercept, emitted_weights):
    strand_lines, span_features, feature_count = homolog_stack_state.shape
    standardized_source = standardize_features(homolog_stack_state.astype(jnp.float32), heeding_normalizer_gains).astype(jnp.bfloat16).reshape(strand_lines * span_features, feature_count)
    packed = jnp.dot(standardized_source, retrieval_weights_qkv, preferred_element_type=jnp.float32).astype(jnp.bfloat16)
    packed = packed.reshape(strand_lines, span_features, 3, HEAD_TOTAL, HEAD_SIZE)
    gate = jax.nn.sigmoid(jnp.dot(standardized_source, logistic_weights, preferred_element_type=jnp.float32) + logistic_intercept.astype(jnp.float32))
    gate = gate.reshape(strand_lines, span_features, feature_count)
    queries = packed[:, :, 0].astype(jnp.float32)
    keys = packed[:, :, 1].astype(jnp.float32)
    values = packed[:, :, 2].astype(jnp.float32)
    logits = jnp.einsum('sthd,uthd->thsu', queries, keys) / math.sqrt(HEAD_SIZE)
    logits = logits + 1000000000.0 * (presence_tally.T[:, None, None, :] - 1.0)
    attn_weights = jax.nn.softmax(logits, axis=-1).astype(jnp.bfloat16)
    mixed = jnp.einsum('thsu,uthd->sthd', attn_weights.astype(jnp.float32), values).reshape(strand_lines, span_features, feature_count)
    gated = (mixed * gate).astype(jnp.bfloat16).reshape(strand_lines * span_features, feature_count)
    increment_terms = jnp.dot(gated, emitted_weights, preferred_element_type=jnp.float32).reshape(strand_lines, span_features, feature_count)
    return (homolog_stack_state.astype(jnp.float32) + increment_terms).astype(jnp.bfloat16)

def map_operand_half(alignment_fresh, presence_tally, gain_vector, weight_matrix):
    strand_lines, span_features, feature_count = alignment_fresh.shape
    standardized_source = standardize_features(alignment_fresh.astype(jnp.float32), gain_vector).astype(jnp.bfloat16).reshape(strand_lines * span_features, feature_count)
    factor = jnp.dot(standardized_source, weight_matrix, preferred_element_type=jnp.float32).reshape(strand_lines, span_features, weight_matrix.shape[1])
    return (factor * presence_tally[:, :, None]).astype(jnp.bfloat16)

def reference(homolog_stack_state, present_flags, chain_ordinal_labels, pairwise_repr, heeding_normalizer_gains, retrieval_weights_qkv, logistic_weights, logistic_intercept, emitted_weights, dyadic_normalizer_gains, former_operand_weights, latter_operand_weights, flattened_outer_projection, clipped_separation_embedding):
    existence_overall = present_flags.astype(jnp.float32)
    homolog_changed = downward_heeding_blend(homolog_stack_state, existence_overall, heeding_normalizer_gains, retrieval_weights_qkv, logistic_weights, logistic_intercept, emitted_weights)
    former_operand = map_operand_half(homolog_changed, existence_overall, dyadic_normalizer_gains, former_operand_weights)
    latter_operand = map_operand_half(homolog_changed, existence_overall, dyadic_normalizer_gains, latter_operand_weights)
    block = math.gcd(STRETCH_SIZE, 64)
    span = 2 * RELPOS_CLIP + 1

    def pair_block(start):
        left_block = lax.dynamic_slice_in_dim(former_operand, start, block, 1)
        outer = jnp.einsum('sic,sje->ijce', left_block.astype(jnp.float32), latter_operand.astype(jnp.float32))
        outer = outer.astype(jnp.bfloat16).reshape(block * STRETCH_SIZE, OPERAND_BREADTH * OPERAND_BREADTH)
        projected = jnp.dot(outer, flattened_outer_projection, preferred_element_type=jnp.float32).reshape(block, STRETCH_SIZE, PAIR_WIDTH)
        mask_block = lax.dynamic_slice_in_dim(existence_overall, start, block, 1)
        counts = jnp.dot(mask_block.T, existence_overall, precision=lax.Precision.HIGHEST)
        residue_block = lax.dynamic_slice_in_dim(chain_ordinal_labels, start, block, 0)
        offsets = jnp.clip(residue_block[:, None] - chain_ordinal_labels[None, :], -RELPOS_CLIP, RELPOS_CLIP) + RELPOS_CLIP
        one_hot = (offsets[:, :, None] == jnp.arange(span, dtype=jnp.int32)[None, None, :]).astype(jnp.bfloat16)
        relpos = jnp.dot(one_hot.reshape(block * STRETCH_SIZE, span), clipped_separation_embedding, preferred_element_type=jnp.float32)
        relpos = relpos.reshape(block, STRETCH_SIZE, PAIR_WIDTH)
        starting_amount = lax.dynamic_slice_in_dim(pairwise_repr, start, block, 0).astype(jnp.float32)
        return (starting_amount + relpos + projected / counts[:, :, None]).astype(jnp.bfloat16)
    starts = jnp.arange(STRETCH_SIZE // block, dtype=jnp.int32) * block
    blocks = lax.map(pair_block, starts)
    couple_state_changed = blocks.reshape(STRETCH_SIZE, STRETCH_SIZE, PAIR_WIDTH)
    return (homolog_changed, couple_state_changed)
```

```python
import functools
import math

import jax
import jax.numpy as jnp
from jax import lax
from jax.experimental import pallas as pl
from jax.experimental.pallas import tpu as pltpu
from jax.sharding import PartitionSpec as P

HEADS = 8
CLIP = 32
HEAD_SIZE = 32
CHUNK = 2
EPS = 1e-05
MESH = pl.DeviceIdType.MESH
F32 = jnp.float32
BF16 = jnp.bfloat16


def mm(a, b):
    return jnp.dot(a, b, preferred_element_type=F32)


def mm_nt(a, b):
    return lax.dot_general(a, b, (((1,), (1,)), ((), ())), preferred_element_type=F32)


def normalise(v, gain):
    mean = jnp.mean(v, axis=-1, keepdims=True)
    centred = v - mean
    var = jnp.mean(centred * centred, axis=-1, keepdims=True)
    return (centred * lax.rsqrt(var + EPS) * gain).astype(BF16)


def kernel(
    n, xs, flags, res_s, res_row, pair, g1, wqkv, wgate, bgate, wout, g2, wl, wr, wp, emb,
    ret, out,
    recv, ybuf, wt, wgb, wk_s, wl4, wrt, mcol, mrow, base, rcount, embp, pmat, rt, rb, obuf,
    a_send, a_recv, r_send, r_recv, g_send, gz, gy, gc,
):
    grp = lax.axis_index("grp")
    me = lax.axis_index("wide")
    tl, _, sl, ch = recv.shape
    tokens = flags.shape[1]
    seqs = flags.shape[0]
    nchunk = tl // CHUNK
    lanes = 128
    width = wl.shape[1]
    per = lanes // width

    barrier = pltpu.get_barrier_semaphore()

    def greet(d, carry):
        p = lax.rem(me + d, n)
        pl.semaphore_signal(barrier, inc=1, device_id=(grp, p), device_id_type=MESH)
        return carry

    lax.fori_loop(1, n, greet, 0)
    pl.semaphore_wait(barrier, n - 1)

    def send_chunk(k):
        part = pl.ds(k * CHUNK, CHUNK)
        pltpu.make_async_copy(xs.at[me, part], recv.at[part, me], a_recv.at[k]).start()

        def one(d, carry):
            p = lax.rem(me + d, n)
            pltpu.make_async_remote_copy(
                src_ref=xs.at[p, part], dst_ref=recv.at[part, me],
                send_sem=a_send, recv_sem=a_recv.at[k],
                device_id=(grp, p), device_id_type=MESH,
            ).start()
            return carry

        lax.fori_loop(1, n, one, 0)

    for k in range(nchunk):
        send_chunk(k)

    for a, src in ((0, wqkv[:, 0:ch]), (1, wqkv[:, 2 * ch : 3 * ch]), (2, wgate[...])):
        wt[a * ch : (a + 1) * ch, :] = src.astype(F32).T.astype(BF16)
    wgb[...] = jnp.broadcast_to(bgate[...], (lanes, ch)).T
    spread = (
        lax.broadcasted_iota(jnp.int32, (width, lanes), 1) % width
        == lax.broadcasted_iota(jnp.int32, (width, lanes), 0)
    ).astype(BF16)
    first = (
        lax.broadcasted_iota(jnp.int32, (width, lanes), 1)
        == lax.broadcasted_iota(jnp.int32, (width, lanes), 0)
    ).astype(BF16)
    wl4[...] = mm(wl[...], spread).astype(BF16)
    wrt[...] = mm(wr[...], first).T[0:width].astype(BF16)
    m_all = flags[...].astype(F32).astype(BF16)
    pick = (
        lax.broadcasted_iota(jnp.int32, (tokens, tl * lanes), 0)
        == me * tl + lax.broadcasted_iota(jnp.int32, (tokens, tl * lanes), 1) // lanes
    ).astype(F32).astype(BF16)
    mine = mm(m_all, pick)
    mcol[...] = mine
    pick8 = (
        lax.broadcasted_iota(jnp.int32, (tl, tokens), 1)
        == me * tl + lax.broadcasted_iota(jnp.int32, (tl, tokens), 0)
    ).astype(F32).astype(BF16)
    mrow[...] = mm_nt(pick8, m_all)
    embp[...] = jnp.zeros_like(embp)
    embp[0 : emb.shape[0], :] = emb[...].astype(F32)
    table = embp[...].astype(BF16)
    mine_b = mine.astype(BF16)
    for jb in range(tokens // lanes):
        js = slice(jb * lanes, (jb + 1) * lanes)
        mt = flags[:, js].astype(F32).T.astype(BF16)
        rcount[js, :] = 1.0 / mm(mt, mine_b)
        res_j = jnp.broadcast_to(res_row[0:1, js], (lanes, lanes)).T
        for i in range(tl):
            off = jnp.clip(res_s[me * tl + i] - res_j, -CLIP, CLIP) + CLIP
            hot = (off == lax.broadcasted_iota(jnp.int32, (lanes, lanes), 1)).astype(F32)
            base[i, js, :] = pair[i, js, :].astype(F32) + mm(hot.astype(BF16), table)

    gain1, gain2 = g1[...], g2[...]
    scale = math.log2(math.e) / math.sqrt(HEAD_SIZE)
    group = lanes // HEAD_SIZE
    lane_block = lax.broadcasted_iota(jnp.int32, (seqs, lanes), 1) // width

    def attend(k, carry):
        part = pl.ds(k * CHUNK, CHUNK)
        pltpu.make_async_copy(recv.at[part], recv.at[part], a_recv.at[k]).wait()
        x = recv[part].astype(F32).reshape(CHUNK * seqs, ch)
        nb = normalise(x, gain1)
        pt = mm_nt(wt[...], nb)
        keys = mm(nb, wqkv[:, ch : 2 * ch]).astype(BF16)
        qt = pt[0:ch].astype(BF16)
        vt = pt[ch : 2 * ch].astype(BF16)
        mixed_parts = []
        for t in range(CHUNK):
            ts = slice(t * seqs, (t + 1) * seqs)
            at = pl.ds(pl.multiple_of((k * CHUNK + t) * lanes, lanes), lanes)
            bias = (mcol[:, at] - 1.0) * 1e9
            gate = jax.nn.sigmoid(pt[2 * ch : 3 * ch, ts] + wgb[...])
            heads = []
            for g in range(HEADS // group):
                kg = keys[ts, g * lanes : (g + 1) * lanes]
                for h in range(group):
                    r = (g * group + h) * HEAD_SIZE
                    pieces = []
                    if h > 0:
                        pieces.append(jnp.zeros((h * HEAD_SIZE, seqs), BF16))
                    pieces.append(qt[r : r + HEAD_SIZE, ts])
                    if h < group - 1:
                        pieces.append(jnp.zeros(((group - 1 - h) * HEAD_SIZE, seqs), BF16))
                    logits = mm(kg, jnp.concatenate(pieces, axis=0)) * scale + bias
                    top = jnp.max(logits, axis=0, keepdims=True)
                    e = jnp.exp2(logits - top)
                    w = (e * (1.0 / jnp.sum(e, axis=0, keepdims=True))).astype(BF16)
                    heads.append(mm(vt[r : r + HEAD_SIZE, ts], w))
            mixed = jnp.concatenate(heads, axis=0)
            mixed_parts.append((mixed * gate).T.astype(BF16))
        gated = jnp.concatenate(mixed_parts, axis=0)
        y = (x + mm(gated, wout[...])).astype(BF16)
        yf = y.astype(F32)
        ybuf[part] = yf.reshape(CHUNK, n, sl, ch).astype(BF16)
        n2 = normalise(yf, gain2)
        left = mm(n2, wl4[...])
        right = mm_nt(wrt[...], n2)
        for t in range(CHUNK):
            ts = slice(t * seqs, (t + 1) * seqs)
            i = k * CHUNK + t
            at = pl.ds(pl.multiple_of(i * lanes, lanes), lanes)
            lt = left[ts] * mcol[:, at]
            for b in range(per):
                pmat[k, b * seqs : (b + 1) * seqs, t * lanes : (t + 1) * lanes] = jnp.where(
                    lane_block == b, lt, 0.0
                ).astype(BF16)
            rt[i] = right[:, ts] * mrow[pl.ds(i, 1), :]
        return carry

    def give_back(k):
        part = pl.ds(k * CHUNK, CHUNK)
        pltpu.make_async_copy(ybuf.at[part, me], ret.at[me, part], r_recv).start()

        def one(d, carry):
            p = lax.rem(me + d, n)
            pltpu.make_async_remote_copy(
                src_ref=ybuf.at[part, p], dst_ref=ret.at[me, part],
                send_sem=r_send, recv_sem=r_recv,
                device_id=(grp, p), device_id_type=MESH,
            ).start()
            return carry

        lax.fori_loop(1, n, one, 0)

    def attend_and_send(k, carry):
        attend(k, 0)
        give_back(k)
        return carry

    lax.fori_loop(0, nchunk - 1, attend_and_send, 0)
    attend(nchunk - 1, 0)

    lines = n // 4
    line, side, core = me // 4, lax.rem(me // 2, 2), lax.rem(me, 2)
    beside = line * 4 + (1 - side) * 2 + core
    twin = line * 4 + side * 2 + (1 - core)
    rb[me] = jnp.swapaxes(rt[...], 0, 1).astype(BF16)

    def push(block, to, sem):
        pltpu.make_async_remote_copy(
            src_ref=rb.at[block], dst_ref=rb.at[block], send_sem=g_send, recv_sem=sem,
            device_id=(grp, to), device_id_type=MESH,
        ).start()

    def along(d, carry):
        to = lax.rem(line + d, lines)
        push(me, to * 4 + side * 2 + core, gz.at[line])
        return carry

    push(me, beside, gy.at[line])
    lax.fori_loop(1, lines, along, 0)
    push(me, twin, gc)
    give_back(nchunk - 1)

    def pass_on(d, carry):
        at = lax.rem(line + d, lines)
        block = at * 4 + side * 2 + core
        pltpu.make_async_copy(rb.at[block], rb.at[block], gz.at[at]).wait()
        push(block, beside, gy.at[at])
        push(block, twin, gc)
        return carry

    lax.fori_loop(1, lines, pass_on, 0)

    def pass_side(d, carry):
        at = lax.rem(line + d, lines)
        block = at * 4 + (1 - side) * 2 + core
        pltpu.make_async_copy(rb.at[block], rb.at[block], gy.at[at]).wait()
        push(block, twin, gc)
        return carry

    lax.fori_loop(0, lines, pass_side, 0)
    half = rb.at[pl.ds(0, n // 2)]
    pltpu.make_async_copy(half, half, gc).wait()

    blocks = lanes // tl

    def pair_block(jb, carry):
        rows = pl.ds(pl.multiple_of(jb * lanes, lanes), lanes)
        for g in range(width // per):
            lhs = jnp.concatenate(
                [
                    rb[pl.ds(jb * blocks, blocks), g * per + b].astype(F32).reshape(lanes, seqs)
                    for b in range(per)
                ],
                axis=1,
            ).astype(BF16)
            for k in range(nchunk):
                o = mm(lhs, pmat[k]).astype(BF16)
                for t in range(CHUNK):
                    obuf[k * CHUNK + t, :, g * lanes : (g + 1) * lanes] = o[
                        :, t * lanes : (t + 1) * lanes
                    ]
        for i in range(tl):
            proj = mm(obuf[i], wp[...])
            out[i, rows, :] = (
                base[i, rows, :] + proj * rcount[rows, i * lanes : (i + 1) * lanes]
            ).astype(BF16)
        return carry

    lax.fori_loop(0, tokens // lanes, pair_block, 0)

    others = xs.at[pl.ds(0, n - 1)]
    pltpu.make_async_copy(others, others, a_send).wait()
    sent = rb.at[pl.ds(0, n - 1)]
    pltpu.make_async_copy(sent, sent, g_send).wait()
    pltpu.make_async_copy(others, others, r_send).wait()
    pltpu.make_async_copy(ret, ret, r_recv).wait()


def on_device(n, x, flags, res, pair, g1, wqkv, wgate, bgate, wout, g2, wl, wr, wp, emb):
    sl, tokens, ch = x.shape
    tl = pair.shape[0]
    seqs = flags.shape[0]
    width = wl.shape[1]
    lanes = 128
    pw = wp.shape[1]
    xs = x.reshape(sl, n, tl, ch).transpose(1, 2, 0, 3)
    wp2 = wp.reshape(width, width, pw).transpose(1, 0, 2).reshape(width * width, pw)
    vmem = pl.BlockSpec(memory_space=pltpu.VMEM)
    anyspace = pl.BlockSpec(memory_space=pl.ANY)
    smem = pl.BlockSpec(memory_space=pltpu.SMEM)
    nchunk = tl // CHUNK
    per = lanes // width
    dma = pltpu.SemaphoreType.DMA
    ret, out = pl.pallas_call(
        functools.partial(kernel, n),
        out_shape=(
            jax.ShapeDtypeStruct((n, tl, sl, ch), BF16),
            jax.ShapeDtypeStruct((tl, tokens, pw), BF16),
        ),
        in_specs=[anyspace, vmem, smem] + [vmem] * 12,
        out_specs=(anyspace, vmem),
        scratch_shapes=[
            pltpu.VMEM((tl, n, sl, ch), BF16),
            pltpu.VMEM((tl, n, sl, ch), BF16),
            pltpu.VMEM((3 * ch, ch), BF16),
            pltpu.VMEM((ch, lanes), F32),
            pltpu.VMEM((8, lanes), F32),
            pltpu.VMEM((ch, lanes), BF16),
            pltpu.VMEM((width, ch), BF16),
            pltpu.VMEM((seqs, tl * lanes), F32),
            pltpu.VMEM((tl, seqs), F32),
            pltpu.VMEM((tl, tokens, pw), F32),
            pltpu.VMEM((tokens, tl * lanes), F32),
            pltpu.VMEM((lanes, pw), F32),
            pltpu.VMEM((nchunk, per * seqs, CHUNK * lanes), BF16),
            pltpu.VMEM((tl, width, seqs), F32),
            pltpu.VMEM((n, width, tl, seqs), BF16),
            pltpu.VMEM((tl, lanes, width * width), BF16),
            dma, dma((nchunk,)), dma, dma, dma, dma((n // 4,)), dma((n // 4,)), dma,
        ],
        compiler_params=pltpu.CompilerParams(
            collective_id=0, has_side_effects=True, vmem_limit_bytes=56 * 1024 * 1024
        ),
        cost_estimate=pl.CostEstimate(
            flops=4 * 10**9, bytes_accessed=4 * 10**6, transcendentals=2 * 10**6
        ),
    )(
        xs, flags, res, res.reshape(1, tokens), pair, g1.reshape(1, ch), wqkv, wgate,
        bgate.reshape(1, ch), wout, g2.reshape(1, ch), wl, wr, wp2, emb,
    )
    changed = ret.transpose(2, 0, 1, 3).reshape(sl, tokens, ch)
    return changed, out


def solution(mesh):
    rows = P(("grp", "wide"), None, None)
    in_specs = (rows, P("grp", None), P("grp"), rows) + (P(),) * 10
    return jax.shard_map(
        functools.partial(on_device, mesh.shape["wide"]), mesh=mesh,
        in_specs=in_specs, out_specs=(rows, rows), check_vma=False,
    )
```
